32 devices in a mesh: dp: 8 (over y, x, core), tensor: 4 (over z).
Axes of the slice: x: 2, y: 2, z: 4, core: 2. Of those that a mesh axis runs over, the one named last changes fastest.
Arguments:
- queries: bfloat16 [2048, 4096], P('dp', 'tensor'), may hold values from -112.5 to 112.5
- token_kv: bfloat16 [2048, 2, 512], P('dp', None, 'tensor'), may hold values from -4.5 to 4.5
- slot_cache: bfloat16 [2048, 2, 512], P('dp', None, 'tensor'), may hold values from -4.5 to 4.5
- lengths: int32 [8], P('dp'), may hold values from 64 to 256, as said below
- upstream: bfloat16 [2048, 8192], P('dp'), may hold values from -36 to 36
- out_weight: bfloat16 [4096, 8192], P('tensor', 'dp'), may hold values from -0.09375 to 0.09375
Outputs:
- layer_output: bfloat16 [2048, 8192], P('dp', 'tensor')
- query_grad: bfloat16 [2048, 4096], P('dp', 'tensor')
- token_kv_grad: bfloat16 [2048, 2, 512], P('dp', None, 'tensor')
- slot_grad: float32 [2048, 2, 512], P('dp', None, 'tensor')
The draws below stay inside these ranges and needn't reach their ends.
Inputs may be any that keep to these rules, and one draw needn't show every extreme that they name: `lengths`: some conversation has exactly 256 real tokens and some exactly 64.
All inputs are finite; a program needn't handle non-finite values.
Results may differ from the reference program's by a relative error of at most 0.012.
The reference program's roundings to bfloat16 on the way count: a program that leaves them out, or rounds other values in their place, can miss the bound.
Values may be sent and summed in bfloat16 or wider, within the bound.
A program may use at most 128 MiB of HBM per device.

```python
import math
import jax
import jax.numpy as jnp
from jax import lax

D = 8192
HD = 128
H = 32
KVH = 4
SLOTS = 2048
LEN = 256
CONV = 8
TOKENS = 2048
N_TENSOR = 4


def slot_base(key):
    return jax.random.truncated_normal(key, -4.5, 4.5, (SLOTS, KVH * HD), jnp.float32)


def draw_slot_cache(key, part):
    key_rows = slot_base(key)
    own_key = jax.random.fold_in(key, 11)
    value_rows = jax.random.truncated_normal(own_key, -4.5, 4.5, (SLOTS, KVH * HD), jnp.float32)
    return jnp.stack([key_rows, value_rows], axis=1).astype(jnp.bfloat16)


def draw_queries(key, part):
    own_key = jax.random.fold_in(key, 23)
    base_rows = jax.random.truncated_normal(own_key, -4.5, 4.5, (TOKENS, H * HD), jnp.float32)
    return base_rows.astype(jnp.bfloat16)


def draw_lengths(key, part):
    key = jax.random.fold_in(key, 31)
    drawn = jax.random.randint(key, (CONV,), LEN // 4, LEN + 1)
    order = jax.random.permutation(jax.random.fold_in(key, 2), CONV)
    drawn = drawn.at[order[0]].set(LEN).at[order[1]].set(LEN // 4)
    return drawn.astype(jnp.int32)


def shard_levels(stream_key, dims, pieces, low, largest):
    loudness = 1.0
    for axis_at, blocks in pieces:
        heights = jax.random.uniform(jax.random.fold_in(jax.random.fold_in(stream_key, 6), axis_at), (blocks,), jnp.float32, low / len(pieces), largest / len(pieces))
        loudness = loudness * jnp.repeat(jnp.exp(heights), dims[axis_at] // blocks).reshape((-1,) + (1,) * (len(dims) - 1 - axis_at))
    return loudness


def gaussian(key, shape, spread, reach, pieces=(), held_as=jnp.bfloat16):
    entries = jax.random.normal(key, shape, jnp.float32) * spread
    if len(pieces) > 0:
        entries = shard_levels(key, shape, pieces, -0.22, 0.18) * entries
    return jnp.clip(entries, min=-reach, max=reach).astype(held_as)


def setup_inputs(seed: int = 0) -> dict:
    seeds = jax.random.split(jax.random.key(seed), 7)
    queries = draw_queries(jax.random.fold_in(seeds[6], 71), 0)
    token_kv = gaussian(seeds[1], (TOKENS, 2, KVH * HD), 1.0, 4.5, ((0, 8), (2, 4)))
    slot_cache = draw_slot_cache(jax.random.fold_in(seeds[6], 71), 0)
    lengths = draw_lengths(jax.random.fold_in(seeds[6], 71), 0)
    upstream = gaussian(seeds[4], (TOKENS, D), 6.0, 36.0, ((0, 8),))
    out_weight = gaussian(seeds[5], (H * HD, D), (H * HD) ** -0.5, 0.09375, ((0, 4), (1, 8)))
    return dict(queries=queries, token_kv=token_kv, slot_cache=slot_cache, lengths=lengths, upstream=upstream, out_weight=out_weight)


def rounded(values):
    return lax.optimization_barrier(values.astype(jnp.bfloat16)).astype(jnp.float32)

def reference(queries, token_kv, slot_cache, lengths, upstream, out_weight):
    score_scale = 1.0 / math.sqrt(HD)
    group_size = H // KVH
    position = jnp.arange(LEN)
    weight_f = out_weight.astype(jnp.float32)

    def attend_one(running, inputs):
        query_rows, token_pairs, length, upstream_rows = inputs
        all_pairs = jnp.concatenate([slot_cache, token_pairs], axis=0).astype(jnp.float32)
        key_heads = all_pairs[:, 0].reshape(-1, KVH, HD)
        value_heads = all_pairs[:, 1].reshape(-1, KVH, HD)
        query_heads = query_rows.astype(jnp.float32).reshape(LEN, KVH, group_size, HD)
        scores = jnp.einsum('tkgd,skd->kgts', query_heads, key_heads) * score_scale
        allowed_tok = (position[None, :] <= position[:, None]) & (position[None, :] < length)
        allowed = jnp.concatenate([jnp.ones((LEN, SLOTS), bool), allowed_tok], axis=1)
        scores = jnp.where(allowed, scores, -jnp.inf)
        row_top = lax.optimization_barrier(jnp.max(scores, axis=-1, keepdims=True))
        shifted = jnp.exp(scores - row_top)
        row_total = lax.optimization_barrier(jnp.sum(shifted, axis=-1, keepdims=True))
        probabilities = shifted / row_total
        weights = rounded(probabilities)
        attended = rounded(jnp.einsum('kgts,skd->tkgd', weights, value_heads)).reshape(LEN, H * HD)
        partial_value = jnp.einsum('tnc,ncd->ntd', attended.reshape(LEN, N_TENSOR, -1), weight_f.reshape(N_TENSOR, -1, D))
        layer_rows = lax.optimization_barrier(jnp.sum(rounded(partial_value), axis=0)).astype(jnp.bfloat16)
        live_rows = position < length
        masked_up = jnp.where(live_rows[:, None], upstream_rows, jnp.zeros_like(upstream_rows))
        out_grad = rounded(jnp.dot(masked_up, out_weight.T, preferred_element_type=jnp.float32))
        grad_heads = out_grad.reshape(LEN, KVH, group_size, HD)
        prob_grad = jnp.einsum('tkgd,skd->kgts', grad_heads, value_heads)
        row_delta = lax.optimization_barrier(jnp.sum(grad_heads * attended.reshape(LEN, KVH, group_size, HD), axis=-1))
        row_delta = jnp.transpose(row_delta, (1, 2, 0))[..., None]
        dscore = rounded(probabilities * (prob_grad - row_delta))
        query_grad = (jnp.einsum('kgts,skd->tkgd', dscore, key_heads) * score_scale).astype(jnp.bfloat16).reshape(LEN, H * HD)
        key_grad = jnp.einsum('kgts,tkgd->skd', dscore, query_heads) * score_scale
        value_grad = jnp.einsum('kgts,tkgd->skd', weights, grad_heads)
        pair_grad = jnp.stack([key_grad, value_grad], axis=1).reshape(SLOTS + LEN, 2, KVH * HD)
        return (running + pair_grad[:SLOTS], (layer_rows, query_grad, pair_grad[SLOTS:].astype(jnp.bfloat16)))
    start_sum = jnp.zeros((SLOTS, 2, KVH * HD), jnp.float32)
    inputs = (queries.reshape(CONV, LEN, H * HD), token_kv.reshape(CONV, LEN, 2, KVH * HD), lengths, upstream.reshape(CONV, LEN, D))
    slot_grad, stacked = lax.scan(attend_one, start_sum, inputs)
    layer_output = stacked[0].reshape(TOKENS, D)
    query_grad = stacked[1].reshape(TOKENS, H * HD)
    token_kv_grad = stacked[2].reshape(TOKENS, 2, KVH * HD)
    return (layer_output, query_grad, token_kv_grad, slot_grad)
```

```python
import functools
import math

import jax
import jax.numpy as jnp
from jax import lax
from jax.experimental import pallas as pl
from jax.experimental.pallas import tpu as pltpu
from jax.sharding import PartitionSpec as P

HD = 128
MESH = pl.DeviceIdType.MESH
NT = (((1,), (1,)), ((), ()))
F32 = jnp.float32
BF16 = jnp.bfloat16
HIDDEN = -1e30


def dot(a, b):
    return jnp.dot(a, b, preferred_element_type=F32)


def dot_nt(a, b):
    return lax.dot_general(a, b, NT, preferred_element_type=F32)


def layer_kernel(
    dp, tn, key_block,
    len_ref, q_ref, tok_ref, slot_ref, up_hbm, w_hbm,
    lo_ref, qg_ref, tg_ref, sg_ref,
    wbuf, up, pbuf, rbuf, kv, kt, vt, q_all, do_all, att, og, dq,
    row_top, row_inv, row_delta, sg_out, sg_in, own_sum, tok_sum,
    load_sem, up_sem, slot_send, slot_fwd, slot_recv, w_send, w_recv,
    z_send, z_recv, g_send, g_recv,
):
    me = lax.axis_index("dp")
    mt = lax.axis_index("tensor")
    rows = q_ref.shape[0]
    heads = q_ref.shape[1] // HD
    own_slots = slot_ref.shape[1]
    slot_count = own_slots * dp
    units = wbuf.shape[1]
    width = wbuf.shape[3]
    cols = units * width
    bits = dp.bit_length() - 1
    per_target = dp // tn
    factor = (1.0 / math.sqrt(HD)) * math.log2(math.e)
    score_scale = 1.0 / math.sqrt(HD)

    def flip(mask):
        total = 0
        for bit in range(bits):
            mine = (me // (1 << bit)) % 2
            theirs = (mask // (1 << bit)) % 2
            total = total + (1 << bit) * ((mine + theirs) % 2)
        return total

    def remote(src, dst, send, recv, dp_index, tensor_index):
        return pltpu.make_async_remote_copy(
            src_ref=src, dst_ref=dst, send_sem=send, recv_sem=recv,
            device_id=(dp_index, tensor_index), device_id_type=MESH,
        )

    loads = []
    for u in range(units):
        loads.append(pltpu.make_async_copy(
            w_hbm.at[:, pl.ds(u * width, width)], wbuf.at[0, u], load_sem.at[u]))
        loads[-1].start()
    up_load = pltpu.make_async_copy(up_hbm, up, up_sem)
    up_load.start()
    kv[:, 0:own_slots, :] = slot_ref[...]
    kv[:, slot_count:slot_count + rows, :] = tok_ref[...]

    barrier = pltpu.get_barrier_semaphore()
    for mask in range(1, dp):
        pl.semaphore_signal(barrier, inc=1, device_id=(flip(mask), mt), device_id_type=MESH)
    for j in range(1, tn):
        pl.semaphore_signal(barrier, inc=1, device_id=(me, (mt + j) % tn), device_id_type=MESH)
    pl.semaphore_wait(barrier, dp + tn - 2)

    def slot_copy(src_mask, dst_mask, send, partner):
        return remote(
            kv.at[:, pl.ds(src_mask * own_slots, own_slots)],
            kv.at[:, pl.ds(dst_mask * own_slots, own_slots)],
            send, slot_recv.at[dst_mask], partner, mt)

    slot_copies = []
    for mask in reversed(range(2, dp, 2)):
        slot_copies.append(slot_copy(0, mask, slot_send.at[mask], flip(mask)))
        slot_copies[-1].start()
    slot_copies.append(slot_copy(0, 1, slot_fwd.at[0], flip(1)))
    slot_copies[-1].start()

    orders = [list(range(1, bits)) + [0], list(range(bits - 1, 0, -1)) + [0]]

    def unit_copy(mask, u, bit):
        return remote(
            wbuf.at[mask, u], wbuf.at[mask + (1 << bit), u],
            w_send.at[mask, u, bit], w_recv.at[mask + (1 << bit), u],
            flip(1 << bit), mt)

    unit_copies = []

    def unit_start(mask, u, bit):
        copy = unit_copy(mask, u, bit)
        copy.start()
        unit_copies.append(copy)

    def group_mask(pos, core, order):
        mask = core
        for stage in range(bits - 1):
            if (pos >> stage) & 1:
                mask += 1 << order[stage]
        return mask

    for load in loads:
        load.wait()
    for stage in range(bits - 1):
        for u in range(units):
            unit_start(0, u, orders[u % 2][stage])

    for mask in range(2, dp, 2):
        slot_copy(0, mask, slot_send.at[mask], flip(mask)).wait_recv()
        slot_copies.append(slot_copy(mask, mask + 1, slot_fwd.at[mask], flip(1)))
        slot_copies[-1].start()
    for u in range(units):
        unit_start(0, u, 0)
    for h in range(heads):
        q_all[h] = q_ref[:, h * HD:(h + 1) * HD]
    for mask in range(1, dp, 2):
        slot_copy(mask - 1, mask, slot_fwd.at[mask - 1], flip(1)).wait_recv()

    for at in range(0, slot_count + rows, key_block):
        size = min(key_block, slot_count + rows - at)
        kt[:, at:at + size] = kv[0, at:at + size, :].astype(F32).T.astype(BF16)
        vt[:, at:at + size] = kv[1, at:at + size, :].astype(F32).T.astype(BF16)

    length = len_ref[0]
    key_at = lax.broadcasted_iota(jnp.int32, (rows, rows), 0)
    query_at = lax.broadcasted_iota(jnp.int32, (rows, rows), 1)

    def token_scores(query):
        scores = dot_nt(kv[0, slot_count:slot_count + rows, :], query)
        return jnp.where((key_at <= query_at) & (key_at < length), scores, HIDDEN)

    @pl.loop(0, heads)
    def _(h):
        query = q_all[h]
        s_slot = dot_nt(kv[0, 0:slot_count, :], query)
        s_tok = token_scores(query)
        top = jnp.maximum(
            jnp.max(s_slot, axis=0, keepdims=True), jnp.max(s_tok, axis=0, keepdims=True))
        e_slot = jnp.exp2((s_slot - top) * factor)
        e_tok = jnp.exp2((s_tok - top) * factor)
        total = jnp.sum(e_slot, axis=0, keepdims=True) + jnp.sum(e_tok, axis=0, keepdims=True)
        inverse = 1.0 / total
        row_top[h] = top
        row_inv[h] = inverse
        out_t = dot(vt[:, 0:slot_count], (e_slot * inverse).astype(BF16))
        out_t += dot(vt[:, slot_count:slot_count + rows], (e_tok * inverse).astype(BF16))
        att[:, pl.ds(pl.multiple_of(h * HD, HD), HD)] = out_t.T.astype(BF16)

    up_load.wait()
    og[...] = jnp.zeros_like(og)

    for pos in range(dp // 2):
        for core in range(2):
            masks = [group_mask(pos, core, order) for order in orders]
            if pos or core:
                for u in range(units):
                    order = orders[u % 2]
                    mask = masks[u % 2]
                    last = max(i for i in range(bits) if (mask >> order[i]) & 1)
                    unit_copy(mask - (1 << order[last]), u, order[last]).wait_recv()
                    for i in range(last + 1, bits):
                        unit_start(mask, u, order[i])

            @pl.loop(0, units)
            def _(u, masks=masks):
                mask = masks[0] + (masks[1] - masks[0]) * (u % 2)
                owner = flip(mask)
                block = wbuf[mask, u]
                target = owner // per_target
                offset = pl.multiple_of((owner % per_target) * cols + u * width, 128)
                pbuf[target, :, pl.ds(offset, width)] = dot(att[...], block).astype(BF16)

                @pl.when(target != mt)
                def _():
                    remote(
                        pbuf.at[target, :, pl.ds(offset, width)],
                        rbuf.at[mt, :, pl.ds(offset, width)],
                        z_send.at[target], z_recv.at[mt], me, target).start()

                start = pl.multiple_of(owner * cols + u * width, 128)
                og[...] += dot_nt(up[:, pl.ds(start, width)], block)

    row_at = lax.broadcasted_iota(jnp.int32, (rows, HD), 0)
    for h in range(heads):
        grad = jnp.where(row_at < length, og[:, h * HD:(h + 1) * HD], 0.0).astype(BF16)
        do_all[h] = grad
        both = grad.astype(F32) * att[:, h * HD:(h + 1) * HD].astype(F32)
        row_delta[h] = jnp.sum(both.T, axis=0, keepdims=True)
    dq[...] = jnp.zeros_like(dq)

    def head_step(h, key, value, key_t, scores, sums):
        query = q_all[h]
        grad = do_all[h]
        prob = jnp.exp2((scores - row_top[h]) * factor) * row_inv[h]
        prob_grad = dot_nt(value, grad)
        dscore = (prob * (prob_grad - row_delta[h])).astype(BF16)
        dq[h] += dot(key_t, dscore)
        key_sum, value_sum = sums
        return key_sum + dot(dscore, query), value_sum + dot(prob.astype(BF16), grad)

    def slot_block(at):
        key = kv[0, pl.ds(at, key_block), :]
        value = kv[1, pl.ds(at, key_block), :]
        key_t = kt[:, pl.ds(at, key_block)]
        zero = jnp.zeros((key_block, HD), F32)

        def step(h, sums):
            return head_step(h, key, value, key_t, dot_nt(key, q_all[h]), sums)

        return lax.fori_loop(0, heads, step, (zero, zero), unroll=2)

    parts = key_block // own_slots

    def grad_copy(mask):
        at = pl.multiple_of(mask * own_slots, 16)
        return remote(
            sg_out.at[:, pl.ds(at, own_slots)], sg_in.at[:, pl.ds(at, own_slots)],
            g_send.at[mask], g_recv.at[mask], flip(mask), mt)

    blocks = slot_count // key_block

    @pl.loop(0, blocks - 1)
    def _(step):
        index = blocks - 1 - step
        at = pl.multiple_of(index * key_block, key_block)
        key_sum, value_sum = slot_block(at)
        sg_out[0, pl.ds(at, key_block), :] = (key_sum * score_scale).astype(BF16)
        sg_out[1, pl.ds(at, key_block), :] = value_sum.astype(BF16)
        for part in range(parts):
            grad_copy(index * parts + part).start()

    key_sum, value_sum = slot_block(0)
    own_sum[0] = key_sum * score_scale
    own_sum[1] = value_sum
    if parts > 1:
        sg_out[:, 0:key_block, :] = own_sum[...].astype(BF16)
        for part in range(1, parts):
            grad_copy(part).start()

    tok_key = kv[0, slot_count:slot_count + rows, :]
    tok_value = kv[1, slot_count:slot_count + rows, :]
    tok_key_t = kt[:, slot_count:slot_count + rows]
    zero = jnp.zeros((rows, HD), F32)

    def tok_step(h, sums):
        return head_step(h, tok_key, tok_value, tok_key_t, token_scores(q_all[h]), sums)

    key_sum, value_sum = lax.fori_loop(0, heads, tok_step, (zero, zero), unroll=2)
    tg_ref[0] = (key_sum * score_scale).astype(BF16)
    tg_ref[1] = value_sum.astype(BF16)

    for h in range(heads):
        qg_ref[:, h * HD:(h + 1) * HD] = (dq[h].T * score_scale).astype(BF16)

    for j in range(1, tn):
        other = (mt + j) % tn
        remote(pbuf.at[other], rbuf.at[other], z_send.at[other], z_recv.at[other], me, other).wait()
    strip = 256

    @pl.loop(0, lo_ref.shape[1] // strip)
    def _(i):
        here = pl.ds(pl.multiple_of(i * strip, strip), strip)
        total = pbuf[mt, :, here].astype(F32)
        for j in range(1, tn):
            total += rbuf[(mt + j) % tn, :, here].astype(F32)
        lo_ref[:, here] = total.astype(BF16)

    total = own_sum[:, 0:own_slots, :]
    for mask in range(1, dp):
        grad_copy(mask).wait()
        total += sg_in[:, mask * own_slots:(mask + 1) * own_slots, :].astype(F32)
    sg_ref[...] = total

    for copy in slot_copies + unit_copies:
        copy.wait_send()


def on_device(dp, tn, queries, token_kv, slot_cache, lengths, upstream, out_weight):
    rows, head_cols = queries.shape
    heads = head_cols // HD
    depth, cols = out_weight.shape
    width = 256 if cols >= 512 else 128
    units = cols // width
    model = upstream.shape[1]
    own_slots = slot_cache.shape[0]
    slot_count = own_slots * dp
    keys = slot_count + rows
    bits = dp.bit_length() - 1
    key_block = max(256, own_slots)
    out_cols = model // tn
    vmem = pl.BlockSpec(memory_space=pltpu.VMEM)
    hbm = pl.BlockSpec(memory_space=pl.ANY)
    dma = pltpu.SemaphoreType.DMA
    outs = pl.pallas_call(
        functools.partial(layer_kernel, dp, tn, key_block),
        out_shape=(
            jax.ShapeDtypeStruct((rows, out_cols), BF16),
            jax.ShapeDtypeStruct((rows, head_cols), BF16),
            jax.ShapeDtypeStruct((2, rows, HD), BF16),
            jax.ShapeDtypeStruct((2, own_slots, HD), F32),
        ),
        in_specs=[pl.BlockSpec(memory_space=pltpu.SMEM), vmem, vmem, vmem, hbm, hbm],
        out_specs=(vmem,) * 4,
        scratch_shapes=[
            pltpu.VMEM((dp, units, depth, width), BF16),
            pltpu.VMEM((rows, model), BF16),
            pltpu.VMEM((tn, rows, out_cols), BF16),
            pltpu.VMEM((tn, rows, out_cols), BF16),
            pltpu.VMEM((2, keys, HD), BF16),
            pltpu.VMEM((HD, keys), BF16),
            pltpu.VMEM((HD, keys), BF16),
            pltpu.VMEM((heads, rows, HD), BF16),
            pltpu.VMEM((heads, rows, HD), BF16),
            pltpu.VMEM((rows, head_cols), BF16),
            pltpu.VMEM((rows, head_cols), F32),
            pltpu.VMEM((heads, HD, rows), F32),
            pltpu.VMEM((heads, 1, rows), F32),
            pltpu.VMEM((heads, 1, rows), F32),
            pltpu.VMEM((heads, 1, rows), F32),
            pltpu.VMEM((2, slot_count, HD), BF16),
            pltpu.VMEM((2, slot_count, HD), BF16),
            pltpu.VMEM((2, key_block, HD), F32),
            pltpu.VMEM((2, rows, HD), F32),
            dma((units,)),
            dma(()),
            dma((dp,)),
            dma((dp,)),
            dma((dp,)),
            dma((dp, units, bits)),
            dma((dp, units)),
            dma((tn,)),
            dma((tn,)),
            dma((dp,)),
            dma((dp,)),
        ],
        compiler_params=pltpu.CompilerParams(
            collective_id=0, has_side_effects=True, vmem_limit_bytes=60 * 1024 * 1024),
        name="layer",
    )(
        lengths, queries, jnp.transpose(token_kv, (1, 0, 2)),
        jnp.transpose(slot_cache, (1, 0, 2)), upstream, out_weight,
    )
    layer_output, query_grad, token_grad, slot_grad = outs
    return (
        layer_output, query_grad,
        jnp.transpose(token_grad, (1, 0, 2)), jnp.transpose(slot_grad, (1, 0, 2)),
    )


def solution(mesh):
    return jax.shard_map(
        functools.partial(on_device, mesh.shape["dp"], mesh.shape["tensor"]),
        mesh=mesh,
        in_specs=(
            P("dp", "tensor"),
            P("dp", None, "tensor"),
            P("dp", None, "tensor"),
            P("dp"),
            P("dp", None),
            P("tensor", "dp"),
        ),
        out_specs=(
            P("dp", "tensor"),
            P("dp", "tensor"),
            P("dp", None, "tensor"),
            P("dp", None, "tensor"),
        ),
        check_vma=False,
    )
```

```python
import functools
import math

import jax
import jax.numpy as jnp
from jax import lax
from jax.experimental import pallas as pl
from jax.experimental.pallas import tpu as pltpu
from jax.sharding import PartitionSpec as P

HD = 128
MESH = pl.DeviceIdType.MESH
NT = (((1,), (1,)), ((), ()))
F32 = jnp.float32
BF16 = jnp.bfloat16
HIDDEN = -1e30


def dot(a, b):
    return jnp.dot(a, b, preferred_element_type=F32)


def dot_nt(a, b):
    return lax.dot_general(a, b, NT, preferred_element_type=F32)


def layer_kernel(
    dp, tn, key_block,
    len_ref, q_ref, tok_ref, slot_ref, up_hbm, w_hbm,
    lo_ref, qg_ref, tg_ref, sg_ref,
    wbuf, up, pbuf, rbuf, kv, kt, vt, q_all, do_all, att, og, dq,
    row_top, row_inv, row_delta, sg_out, sg_in, own_sum,
    load_sem, up_sem, slot_send, slot_fwd, slot_recv, w_send, w_recv,
    z_send, z_recv, g_send, g_recv,
):
    me = lax.axis_index("dp")
    mt = lax.axis_index("tensor")
    rows = q_ref.shape[0]
    heads = q_ref.shape[1] // HD
    own_slots = slot_ref.shape[1]
    slot_count = own_slots * dp
    units = wbuf.shape[1]
    width = wbuf.shape[3]
    cols = units * width
    bits = dp.bit_length() - 1
    per_target = dp // tn
    factor = (1.0 / math.sqrt(HD)) * math.log2(math.e)
    score_scale = 1.0 / math.sqrt(HD)

    def flip(mask):
        total = 0
        for bit in range(bits):
            mine = (me // (1 << bit)) % 2
            theirs = (mask // (1 << bit)) % 2
            total = total + (1 << bit) * ((mine + theirs) % 2)
        return total

    def remote(src, dst, send, recv, dp_index, tensor_index):
        return pltpu.make_async_remote_copy(
            src_ref=src, dst_ref=dst, send_sem=send, recv_sem=recv,
            device_id=(dp_index, tensor_index), device_id_type=MESH,
        )

    loads = []
    for u in range(units):
        loads.append(pltpu.make_async_copy(
            w_hbm.at[:, pl.ds(u * width, width)], wbuf.at[0, u], load_sem.at[u]))
        loads[-1].start()
    up_load = pltpu.make_async_copy(up_hbm, up, up_sem)
    up_load.start()
    kv[:, 0:own_slots, :] = slot_ref[...]
    kv[:, slot_count:slot_count + rows, :] = tok_ref[...]

    barrier = pltpu.get_barrier_semaphore()
    for mask in range(1, dp):
        pl.semaphore_signal(barrier, inc=1, device_id=(flip(mask), mt), device_id_type=MESH)
    for j in range(1, tn):
        pl.semaphore_signal(barrier, inc=1, device_id=(me, (mt + j) % tn), device_id_type=MESH)
    pl.semaphore_wait(barrier, dp + tn - 2)

    @pl.when(mt == 0)
    def _():
        rbuf[0] = jnp.zeros(rbuf.shape[1:], BF16)

    @pl.when(mt == tn - 1)
    def _():
        rbuf[tn] = jnp.zeros(rbuf.shape[1:], BF16)

    def slot_copy(src_mask, dst_mask, send, partner):
        return remote(
            kv.at[:, pl.ds(src_mask * own_slots, own_slots)],
            kv.at[:, pl.ds(dst_mask * own_slots, own_slots)],
            send, slot_recv.at[dst_mask], partner, mt)

    slot_copies = []
    for mask in reversed(range(2, dp, 2)):
        slot_copies.append(slot_copy(0, mask, slot_send.at[mask], flip(mask)))
        slot_copies[-1].start()
    slot_copies.append(slot_copy(0, 1, slot_fwd.at[0], flip(1)))
    slot_copies[-1].start()

    orders = [list(range(1, bits)) + [0], list(range(bits - 1, 0, -1)) + [0]]

    def unit_copy(mask, u, bit):
        return remote(
            wbuf.at[mask, u], wbuf.at[mask + (1 << bit), u],
            w_send.at[mask, u, bit], w_recv.at[mask + (1 << bit), u],
            flip(1 << bit), mt)

    unit_copies = []

    def unit_start(mask, u, bit):
        copy = unit_copy(mask, u, bit)
        copy.start()
        unit_copies.append(copy)

    def group_mask(pos, core, order):
        mask = core
        for stage in range(bits - 1):
            if (pos >> stage) & 1:
                mask += 1 << order[stage]
        return mask

    for load in loads:
        load.wait()
    for stage in range(bits - 1):
        for u in range(units):
            unit_start(0, u, orders[u % 2][stage])

    for mask in range(2, dp, 2):
        slot_copy(0, mask, slot_send.at[mask], flip(mask)).wait_recv()
        slot_copies.append(slot_copy(mask, mask + 1, slot_fwd.at[mask], flip(1)))
        slot_copies[-1].start()
    for u in range(units):
        unit_start(0, u, 0)
    for h in range(heads):
        q_all[h] = q_ref[:, h * HD:(h + 1) * HD]
    for mask in range(1, dp, 2):
        slot_copy(mask - 1, mask, slot_fwd.at[mask - 1], flip(1)).wait_recv()

    for at in range(0, slot_count + rows, key_block):
        size = min(key_block, slot_count + rows - at)
        kt[:, at:at + size] = kv[0, at:at + size, :].astype(F32).T.astype(BF16)
        vt[:, at:at + size] = kv[1, at:at + size, :].astype(F32).T.astype(BF16)

    length = len_ref[0]
    key_at = lax.broadcasted_iota(jnp.int32, (rows, rows), 0)
    query_at = lax.broadcasted_iota(jnp.int32, (rows, rows), 1)

    def token_scores(query):
        scores = dot_nt(kv[0, slot_count:slot_count + rows, :], query)
        return jnp.where((key_at <= query_at) & (key_at < length), scores, HIDDEN)

    @pl.loop(0, heads)
    def _(h):
        query = q_all[h]
        s_slot = dot_nt(kv[0, 0:slot_count, :], query)
        s_tok = token_scores(query)
        top = jnp.maximum(
            jnp.max(s_slot, axis=0, keepdims=True), jnp.max(s_tok, axis=0, keepdims=True))
        e_slot = jnp.exp2((s_slot - top) * factor)
        e_tok = jnp.exp2((s_tok - top) * factor)
        total = jnp.sum(e_slot, axis=0, keepdims=True) + jnp.sum(e_tok, axis=0, keepdims=True)
        inverse = 1.0 / total
        row_top[h] = top
        row_inv[h] = inverse
        out_t = dot(vt[:, 0:slot_count], (e_slot * inverse).astype(BF16))
        out_t += dot(vt[:, slot_count:slot_count + rows], (e_tok * inverse).astype(BF16))
        att[:, pl.ds(pl.multiple_of(h * HD, HD), HD)] = out_t.T.astype(BF16)

    up_load.wait()
    og[...] = jnp.zeros_like(og)

    unit_total = dp * units
    lag = 2 * units

    def unit_at(step):
        group, u = step // units, step % units
        pos, core = group // 2, group % 2
        masks = []
        for order in orders:
            mask = core
            for stage in range(bits - 1):
                mask = mask + (1 << order[stage]) * ((pos // (1 << stage)) % 2)
            masks.append(mask)
        mask = masks[0] + (masks[1] - masks[0]) * (u % 2)
        owner = flip(mask)
        target = owner // per_target
        offset = pl.multiple_of((owner % per_target) * cols + u * width, 128)
        return mask, u, owner, target, offset, (owner % per_target) * units + u

    def relay(step, up_way):
        _, _, _, target, offset, index = unit_at(step)
        here = (target, slice(None), pl.ds(offset, width))
        first = (mt == 0) if up_way else (mt == tn - 1)
        partner = mt + 1 if up_way else mt - 1

        @pl.when((target > mt) if up_way else (target < mt))
        def _():
            @pl.when(jnp.logical_not(first))
            def _():
                remote(
                    pbuf.at[here], rbuf.at[here], z_send.at[target],
                    z_recv.at[target, index], me, partner).wait_recv()
                pbuf[here] = (pbuf[here].astype(F32) + rbuf[here].astype(F32)).astype(BF16)

            if up_way:
                slot = target
            else:
                slot = jnp.where(partner == target, tn, target)
            remote(
                pbuf.at[here], rbuf.at[slot, :, pl.ds(offset, width)],
                z_send.at[target], z_recv.at[slot, index], me, partner).start()

    def relay_step(step):
        for up_way in (True, False):
            late = step - lag * (mt if up_way else tn - 1 - mt)

            @pl.when((late >= 0) & (late < unit_total))
            def _(late=late, up_way=up_way):
                relay(late, up_way)

    for pos in range(dp // 2):
        for core in range(2):
            masks = [group_mask(pos, core, order) for order in orders]
            if pos or core:
                for u in range(units):
                    order = orders[u % 2]
                    mask = masks[u % 2]
                    last = max(i for i in range(bits) if (mask >> order[i]) & 1)
                    unit_copy(mask - (1 << order[last]), u, order[last]).wait_recv()
                    for i in range(last + 1, bits):
                        unit_start(mask, u, order[i])

            @pl.loop(0, units)
            def _(u, group=2 * pos + core):
                step = group * units + u
                mask, _, owner, target, offset, _ = unit_at(step)
                block = wbuf[mask, u]
                pbuf[target, :, pl.ds(offset, width)] = dot(att[...], block).astype(BF16)
                start = pl.multiple_of(owner * cols + u * width, 128)
                relay_step(step)
                og[...] += dot_nt(up[:, pl.ds(start, width)], block)

    row_at = lax.broadcasted_iota(jnp.int32, (rows, HD), 0)
    for h in range(heads):
        grad = jnp.where(row_at < length, og[:, h * HD:(h + 1) * HD], 0.0).astype(BF16)
        do_all[h] = grad
        both = grad.astype(F32) * att[:, h * HD:(h + 1) * HD].astype(F32)
        row_delta[h] = jnp.sum(both.T, axis=0, keepdims=True)
    dq[...] = jnp.zeros_like(dq)

    def head_step(h, key, value, key_t, scores, sums):
        query = q_all[h]
        grad = do_all[h]
        prob = jnp.exp2((scores - row_top[h]) * factor) * row_inv[h]
        prob_grad = dot_nt(value, grad)
        dscore = (prob * (prob_grad - row_delta[h])).astype(BF16)
        dq[h] += dot(key_t, dscore)
        key_sum, value_sum = sums
        return key_sum + dot(dscore, query), value_sum + dot(prob.astype(BF16), grad)

    def slot_block(at):
        key = kv[0, pl.ds(at, key_block), :]
        value = kv[1, pl.ds(at, key_block), :]
        key_t = kt[:, pl.ds(at, key_block)]
        zero = jnp.zeros((key_block, HD), F32)

        def step(h, sums):
            return head_step(h, key, value, key_t, dot_nt(key, q_all[h]), sums)

        return lax.fori_loop(0, heads, step, (zero, zero), unroll=2)

    parts = key_block // own_slots

    def grad_copy(mask):
        at = pl.multiple_of(mask * own_slots, 16)
        return remote(
            sg_out.at[:, pl.ds(at, own_slots)], sg_in.at[:, pl.ds(at, own_slots)],
            g_send.at[mask], g_recv.at[mask], flip(mask), mt)

    blocks = slot_count // key_block
    late_steps = -(-lag * (tn - 2) // (blocks - 1))

    @pl.loop(0, blocks - 1)
    def _(step):
        index = blocks - 1 - step
        at = pl.multiple_of(index * key_block, key_block)
        key_sum, value_sum = slot_block(at)
        sg_out[0, pl.ds(at, key_block), :] = (key_sum * score_scale).astype(BF16)
        sg_out[1, pl.ds(at, key_block), :] = value_sum.astype(BF16)
        for part in range(parts):
            grad_copy(index * parts + part).start()
        for i in range(late_steps):
            relay_step(unit_total + step * late_steps + i)

    key_sum, value_sum = slot_block(0)
    own_sum[0] = key_sum * score_scale
    own_sum[1] = value_sum
    if parts > 1:
        sg_out[:, 0:key_block, :] = own_sum[...].astype(BF16)
        for part in range(1, parts):
            grad_copy(part).start()

    tok_key = kv[0, slot_count:slot_count + rows, :]
    tok_value = kv[1, slot_count:slot_count + rows, :]
    tok_key_t = kt[:, slot_count:slot_count + rows]
    zero = jnp.zeros((rows, HD), F32)

    def tok_step(h, sums):
        return head_step(h, tok_key, tok_value, tok_key_t, token_scores(q_all[h]), sums)

    key_sum, value_sum = lax.fori_loop(0, heads, tok_step, (zero, zero), unroll=2)
    tg_ref[0] = (key_sum * score_scale).astype(BF16)
    tg_ref[1] = value_sum.astype(BF16)

    for h in range(heads):
        qg_ref[:, h * HD:(h + 1) * HD] = (dq[h].T * score_scale).astype(BF16)

    def collect(slot):
        @pl.loop(0, per_target * units)
        def _(index):
            here = (slot, slice(None), pl.ds(pl.multiple_of(index * width, 128), width))
            remote(
                pbuf.at[0, :, pl.ds(0, width)], rbuf.at[here], z_send.at[0],
                z_recv.at[slot, index], me, (mt + 1) % tn).wait_recv()

    @pl.when(mt > 0)
    def _():
        collect(mt)

    @pl.when(mt < tn - 1)
    def _():
        collect(tn)

    strip = 256

    @pl.loop(0, lo_ref.shape[1] // strip)
    def _(i):
        here = pl.ds(pl.multiple_of(i * strip, strip), strip)
        total = pbuf[mt, :, here].astype(F32)
        total += rbuf[mt, :, here].astype(F32) + rbuf[tn, :, here].astype(F32)
        lo_ref[:, here] = total.astype(BF16)

    total = own_sum[:, 0:own_slots, :]
    for mask in range(1, dp):
        grad_copy(mask).wait()
        total += sg_in[:, mask * own_slots:(mask + 1) * own_slots, :].astype(F32)
    sg_ref[...] = total

    for copy in slot_copies + unit_copies:
        copy.wait_send()
    for j in range(1, tn):
        other = (mt + j) % tn
        remote(
            pbuf.at[other], rbuf.at[other], z_send.at[other],
            z_recv.at[other, 0], me, other).wait_send()


def on_device(dp, tn, queries, token_kv, slot_cache, lengths, upstream, out_weight):
    rows, head_cols = queries.shape
    heads = head_cols // HD
    depth, cols = out_weight.shape
    width = 256 if cols >= 512 else 128
    units = cols // width
    model = upstream.shape[1]
    own_slots = slot_cache.shape[0]
    slot_count = own_slots * dp
    keys = slot_count + rows
    bits = dp.bit_length() - 1
    key_block = max(256, own_slots)
    out_cols = model // tn
    vmem = pl.BlockSpec(memory_space=pltpu.VMEM)
    hbm = pl.BlockSpec(memory_space=pl.ANY)
    dma = pltpu.SemaphoreType.DMA
    outs = pl.pallas_call(
        functools.partial(layer_kernel, dp, tn, key_block),
        out_shape=(
            jax.ShapeDtypeStruct((rows, out_cols), BF16),
            jax.ShapeDtypeStruct((rows, head_cols), BF16),
            jax.ShapeDtypeStruct((2, rows, HD), BF16),
            jax.ShapeDtypeStruct((2, own_slots, HD), F32),
        ),
        in_specs=[pl.BlockSpec(memory_space=pltpu.SMEM), vmem, vmem, vmem, hbm, hbm],
        out_specs=(vmem,) * 4,
        scratch_shapes=[
            pltpu.VMEM((dp, units, depth, width), BF16),
            pltpu.VMEM((rows, model), BF16),
            pltpu.VMEM((tn, rows, out_cols), BF16),
            pltpu.VMEM((tn + 1, rows, out_cols), BF16),
            pltpu.VMEM((2, keys, HD), BF16),
            pltpu.VMEM((HD, keys), BF16),
            pltpu.VMEM((HD, keys), BF16),
            pltpu.VMEM((heads, rows, HD), BF16),
            pltpu.VMEM((heads, rows, HD), BF16),
            pltpu.VMEM((rows, head_cols), BF16),
            pltpu.VMEM((rows, head_cols), F32),
            pltpu.VMEM((heads, HD, rows), F32),
            pltpu.VMEM((heads, 1, rows), F32),
            pltpu.VMEM((heads, 1, rows), F32),
            pltpu.VMEM((heads, 1, rows), F32),
            pltpu.VMEM((2, slot_count, HD), BF16),
            pltpu.VMEM((2, slot_count, HD), BF16),
            pltpu.VMEM((2, key_block, HD), F32),
            dma((units,)),
            dma(()),
            dma((dp,)),
            dma((dp,)),
            dma((dp,)),
            dma((dp, units, bits)),
            dma((dp, units)),
            dma((tn,)),
            dma((tn + 1, dp // tn * units)),
            dma((dp,)),
            dma((dp,)),
        ],
        compiler_params=pltpu.CompilerParams(
            collective_id=0, has_side_effects=True, vmem_limit_bytes=60 * 1024 * 1024),
        name="layer",
    )(
        lengths, queries, jnp.transpose(token_kv, (1, 0, 2)),
        jnp.transpose(slot_cache, (1, 0, 2)), upstream, out_weight,
    )
    layer_output, query_grad, token_grad, slot_grad = outs
    return (
        layer_output, query_grad,
        jnp.transpose(token_grad, (1, 0, 2)), jnp.transpose(slot_grad, (1, 0, 2)),
    )


def solution(mesh):
    return jax.shard_map(
        functools.partial(on_device, mesh.shape["dp"], mesh.shape["tensor"]),
        mesh=mesh,
        in_specs=(
            P("dp", "tensor"),
            P("dp", None, "tensor"),
            P("dp", None, "tensor"),
            P("dp"),
            P("dp", None),
            P("tensor", "dp"),
        ),
        out_specs=(
            P("dp", "tensor"),
            P("dp", "tensor"),
            P("dp", None, "tensor"),
            P("dp", None, "tensor"),
        ),
        check_vma=False,
    )
```

```python
import functools
import math

import jax
import jax.numpy as jnp
from jax import lax
from jax.experimental import pallas as pl
from jax.experimental.pallas import tpu as pltpu
from jax.sharding import PartitionSpec as P

HD = 128
MESH = pl.DeviceIdType.MESH
NT = (((1,), (1,)), ((), ()))
F32 = jnp.float32
BF16 = jnp.bfloat16
HIDDEN = -1e30


def dot(a, b):
    return jnp.dot(a, b, preferred_element_type=F32)


def dot_nt(a, b):
    return lax.dot_general(a, b, NT, preferred_element_type=F32)


def layer_kernel(
    dp, tn, key_block,
    len_ref, q_ref, tok_ref, slot_ref, up_hbm, w_hbm,
    lo_ref, qg_ref, tg_ref, sg_ref,
    wbuf, up, pbuf, rbuf, kv, kt, vt, q_all, do_all, att, og, dq,
    row_top, row_inv, row_delta, sg_out, sg_in, own_sum,
    load_sem, up_sem, slot_send, slot_fwd, slot_recv, w_send, w_recv,
    z_send, z_recv, g_send, g_recv,
):
    me = lax.axis_index("dp")
    mt = lax.axis_index("tensor")
    rows = q_ref.shape[0]
    heads = q_ref.shape[1] // HD
    own_slots = slot_ref.shape[1]
    slot_count = own_slots * dp
    units = wbuf.shape[1]
    width = wbuf.shape[3]
    cols = units * width
    bits = dp.bit_length() - 1
    per_target = dp // tn
    factor = (1.0 / math.sqrt(HD)) * math.log2(math.e)
    score_scale = 1.0 / math.sqrt(HD)

    def flip(mask):
        total = 0
        for bit in range(bits):
            mine = (me // (1 << bit)) % 2
            theirs = (mask // (1 << bit)) % 2
            total = total + (1 << bit) * ((mine + theirs) % 2)
        return total

    def remote(src, dst, send, recv, dp_index, tensor_index):
        return pltpu.make_async_remote_copy(
            src_ref=src, dst_ref=dst, send_sem=send, recv_sem=recv,
            device_id=(dp_index, tensor_index), device_id_type=MESH,
        )

    loads = []
    for u in range(units):
        loads.append(pltpu.make_async_copy(
            w_hbm.at[:, pl.ds(u * width, width)], wbuf.at[0, u], load_sem.at[u]))
        loads[-1].start()
    up_load = pltpu.make_async_copy(up_hbm, up, up_sem)
    up_load.start()
    kv[:, 0:own_slots, :] = slot_ref[...]
    kv[:, slot_count:slot_count + rows, :] = tok_ref[...]

    barrier = pltpu.get_barrier_semaphore()
    for mask in range(1, dp):
        pl.semaphore_signal(barrier, inc=1, device_id=(flip(mask), mt), device_id_type=MESH)
    for j in range(1, tn):
        pl.semaphore_signal(barrier, inc=1, device_id=(me, (mt + j) % tn), device_id_type=MESH)
    pl.semaphore_wait(barrier, dp + tn - 2)

    @pl.when(mt == 0)
    def _():
        rbuf[0] = jnp.zeros(rbuf.shape[1:], BF16)

    @pl.when(mt == tn - 1)
    def _():
        rbuf[tn] = jnp.zeros(rbuf.shape[1:], BF16)

    def slot_copy(src_mask, dst_mask, send, partner):
        return remote(
            kv.at[:, pl.ds(src_mask * own_slots, own_slots)],
            kv.at[:, pl.ds(dst_mask * own_slots, own_slots)],
            send, slot_recv.at[dst_mask], partner, mt)

    slot_copies = []
    for mask in reversed(range(2, dp, 2)):
        slot_copies.append(slot_copy(0, mask, slot_send.at[mask], flip(mask)))
        slot_copies[-1].start()
    slot_copies.append(slot_copy(0, 1, slot_fwd.at[0], flip(1)))
    slot_copies[-1].start()

    orders = [list(range(1, bits)) + [0], list(range(bits - 1, 0, -1)) + [0]]

    def unit_copy(mask, u, bit):
        return remote(
            wbuf.at[mask, u], wbuf.at[mask + (1 << bit), u],
            w_send.at[mask, u, bit], w_recv.at[mask + (1 << bit), u],
            flip(1 << bit), mt)

    unit_copies = []

    def unit_start(mask, u, bit):
        copy = unit_copy(mask, u, bit)
        copy.start()
        unit_copies.append(copy)

    def group_mask(pos, core, order):
        mask = core
        for stage in range(bits - 1):
            if (pos >> stage) & 1:
                mask += 1 << order[stage]
        return mask

    for load in loads:
        load.wait()
    for stage in range(bits - 1):
        for u in range(units):
            unit_start(0, u, orders[u % 2][stage])

    for mask in range(2, dp, 2):
        slot_copy(0, mask, slot_send.at[mask], flip(mask)).wait_recv()
        slot_copies.append(slot_copy(mask, mask + 1, slot_fwd.at[mask], flip(1)))
        slot_copies[-1].start()
    for u in range(units):
        unit_start(0, u, 0)
    for h in range(heads):
        q_all[h] = q_ref[:, h * HD:(h + 1) * HD]
    for mask in range(1, dp, 2):
        slot_copy(mask - 1, mask, slot_fwd.at[mask - 1], flip(1)).wait_recv()

    for at in range(0, slot_count + rows, key_block):
        size = min(key_block, slot_count + rows - at)
        kt[:, at:at + size] = kv[0, at:at + size, :].astype(F32).T.astype(BF16)
        vt[:, at:at + size] = kv[1, at:at + size, :].astype(F32).T.astype(BF16)

    length = len_ref[0]
    key_at = lax.broadcasted_iota(jnp.int32, (rows, rows), 0)
    query_at = lax.broadcasted_iota(jnp.int32, (rows, rows), 1)

    def token_scores(query):
        scores = dot_nt(kv[0, slot_count:slot_count + rows, :], query)
        return jnp.where((key_at <= query_at) & (key_at < length), scores, HIDDEN)

    @pl.loop(0, heads)
    def _(h):
        query = q_all[h]
        s_slot = dot_nt(kv[0, 0:slot_count, :], query)
        s_tok = token_scores(query)
        top = jnp.maximum(
            jnp.max(s_slot, axis=0, keepdims=True), jnp.max(s_tok, axis=0, keepdims=True))
        e_slot = jnp.exp2((s_slot - top) * factor)
        e_tok = jnp.exp2((s_tok - top) * factor)
        total = jnp.sum(e_slot, axis=0, keepdims=True) + jnp.sum(e_tok, axis=0, keepdims=True)
        inverse = 1.0 / total
        row_top[h] = top
        row_inv[h] = inverse
        out_t = dot(vt[:, 0:slot_count], (e_slot * inverse).astype(BF16))
        out_t += dot(vt[:, slot_count:slot_count + rows], (e_tok * inverse).astype(BF16))
        att[:, pl.ds(pl.multiple_of(h * HD, HD), HD)] = out_t.T.astype(BF16)

    up_load.wait()
    og[...] = jnp.zeros_like(og)

    unit_total = dp * units
    lag = 2 * units

    def unit_at(step):
        group, u = step // units, step % units
        pos, core = group // 2, group % 2
        masks = []
        for order in orders:
            mask = core
            for stage in range(bits - 1):
                mask = mask + (1 << order[stage]) * ((pos // (1 << stage)) % 2)
            masks.append(mask)
        mask = masks[0] + (masks[1] - masks[0]) * (u % 2)
        owner = flip(mask)
        target = owner // per_target
        offset = pl.multiple_of((owner % per_target) * cols + u * width, 128)
        return mask, u, owner, target, offset, (owner % per_target) * units + u

    def relay(step, up_way):
        _, _, _, target, offset, index = unit_at(step)
        here = (target, slice(None), pl.ds(offset, width))
        first = (mt == 0) if up_way else (mt == tn - 1)
        partner = mt + 1 if up_way else mt - 1

        @pl.when((target > mt) if up_way else (target < mt))
        def _():
            @pl.when(jnp.logical_not(first))
            def _():
                remote(
                    pbuf.at[here], rbuf.at[here], z_send.at[target],
                    z_recv.at[target, index], me, partner).wait_recv()
                pbuf[here] = (pbuf[here].astype(F32) + rbuf[here].astype(F32)).astype(BF16)

            if up_way:
                slot = target
            else:
                slot = jnp.where(partner == target, tn, target)
            remote(
                pbuf.at[here], rbuf.at[slot, :, pl.ds(offset, width)],
                z_send.at[target], z_recv.at[slot, index], me, partner).start()

    def relay_step(step):
        for up_way in (True, False):
            late = step - lag * (mt if up_way else tn - 1 - mt)

            @pl.when((late >= 0) & (late < unit_total))
            def _(late=late, up_way=up_way):
                relay(late, up_way)

    for pos in range(dp // 2):
        for core in range(2):
            masks = [group_mask(pos, core, order) for order in orders]
            if pos or core:
                for u in range(units):
                    order = orders[u % 2]
                    mask = masks[u % 2]
                    last = max(i for i in range(bits) if (mask >> order[i]) & 1)
                    unit_copy(mask - (1 << order[last]), u, order[last]).wait_recv()
                    for i in range(last + 1, bits):
                        unit_start(mask, u, order[i])

            @pl.loop(0, units)
            def _(u, group=2 * pos + core):
                step = group * units + u
                mask, _, owner, target, offset, _ = unit_at(step)
                block = wbuf[mask, u]
                pbuf[target, :, pl.ds(offset, width)] = dot(att[...], block).astype(BF16)
                start = pl.multiple_of(owner * cols + u * width, 128)
                og[...] += dot_nt(up[:, pl.ds(start, width)], block)
                relay_step(step)

    row_at = lax.broadcasted_iota(jnp.int32, (rows, HD), 0)
    for h in range(heads):
        grad = jnp.where(row_at < length, og[:, h * HD:(h + 1) * HD], 0.0).astype(BF16)
        do_all[h] = grad
        both = grad.astype(F32) * att[:, h * HD:(h + 1) * HD].astype(F32)
        row_delta[h] = jnp.sum(both.T, axis=0, keepdims=True)
    dq[...] = jnp.zeros_like(dq)

    def head_step(h, key, value, key_t, scores, sums):
        query = q_all[h]
        grad = do_all[h]
        prob = jnp.exp2((scores - row_top[h]) * factor) * row_inv[h]
        prob_grad = dot_nt(value, grad)
        dscore = (prob * (prob_grad - row_delta[h])).astype(BF16)
        dq[h] += dot(key_t, dscore)
        key_sum, value_sum = sums
        return key_sum + dot(dscore, query), value_sum + dot(prob.astype(BF16), grad)

    def slot_block(at):
        key = kv[0, pl.ds(at, key_block), :]
        value = kv[1, pl.ds(at, key_block), :]
        key_t = kt[:, pl.ds(at, key_block)]
        zero = jnp.zeros((key_block, HD), F32)

        def step(h, sums):
            return head_step(h, key, value, key_t, dot_nt(key, q_all[h]), sums)

        return lax.fori_loop(0, heads, step, (zero, zero), unroll=2)

    parts = key_block // own_slots

    def grad_copy(mask):
        at = pl.multiple_of(mask * own_slots, 16)
        return remote(
            sg_out.at[:, pl.ds(at, own_slots)], sg_in.at[:, pl.ds(at, own_slots)],
            g_send.at[mask], g_recv.at[mask], flip(mask), mt)

    blocks = slot_count // key_block
    late_steps = -(-lag * (tn - 2) // (blocks - 1))

    @pl.loop(0, blocks - 1)
    def _(step):
        index = blocks - 1 - step
        at = pl.multiple_of(index * key_block, key_block)
        key_sum, value_sum = slot_block(at)
        sg_out[0, pl.ds(at, key_block), :] = (key_sum * score_scale).astype(BF16)
        sg_out[1, pl.ds(at, key_block), :] = value_sum.astype(BF16)
        for part in range(parts):
            grad_copy(index * parts + part).start()
        for i in range(late_steps):
            relay_step(unit_total + step * late_steps + i)

    key_sum, value_sum = slot_block(0)
    own_sum[0] = key_sum * score_scale
    own_sum[1] = value_sum
    if parts > 1:
        sg_out[:, 0:key_block, :] = own_sum[...].astype(BF16)
        for part in range(1, parts):
            grad_copy(part).start()

    tok_key = kv[0, slot_count:slot_count + rows, :]
    tok_value = kv[1, slot_count:slot_count + rows, :]
    tok_key_t = kt[:, slot_count:slot_count + rows]
    zero = jnp.zeros((rows, HD), F32)

    def tok_step(h, sums):
        return head_step(h, tok_key, tok_value, tok_key_t, token_scores(q_all[h]), sums)

    key_sum, value_sum = lax.fori_loop(0, heads, tok_step, (zero, zero), unroll=2)
    tg_ref[0] = (key_sum * score_scale).astype(BF16)
    tg_ref[1] = value_sum.astype(BF16)

    for h in range(heads):
        qg_ref[:, h * HD:(h + 1) * HD] = (dq[h].T * score_scale).astype(BF16)

    def collect(slot):
        @pl.loop(0, per_target * units)
        def _(index):
            here = (slot, slice(None), pl.ds(pl.multiple_of(index * width, 128), width))
            remote(
                pbuf.at[0, :, pl.ds(0, width)], rbuf.at[here], z_send.at[0],
                z_recv.at[slot, index], me, (mt + 1) % tn).wait_recv()

    @pl.when(mt > 0)
    def _():
        collect(mt)

    @pl.when(mt < tn - 1)
    def _():
        collect(tn)

    strip = 256

    @pl.loop(0, lo_ref.shape[1] // strip)
    def _(i):
        here = pl.ds(pl.multiple_of(i * strip, strip), strip)
        total = pbuf[mt, :, here].astype(F32)
        total += rbuf[mt, :, here].astype(F32) + rbuf[tn, :, here].astype(F32)
        lo_ref[:, here] = total.astype(BF16)

    total = own_sum[:, 0:own_slots, :]
    for mask in range(1, dp):
        grad_copy(mask).wait()
        total += sg_in[:, mask * own_slots:(mask + 1) * own_slots, :].astype(F32)
    sg_ref[...] = total

    for copy in slot_copies + unit_copies:
        copy.wait_send()
    for j in range(1, tn):
        other = (mt + j) % tn
        remote(
            pbuf.at[other], rbuf.at[other], z_send.at[other],
            z_recv.at[other, 0], me, other).wait_send()


def on_device(dp, tn, queries, token_kv, slot_cache, lengths, upstream, out_weight):
    rows, head_cols = queries.shape
    heads = head_cols // HD
    depth, cols = out_weight.shape
    width = 256 if cols >= 512 else 128
    units = cols // width
    model = upstream.shape[1]
    own_slots = slot_cache.shape[0]
    slot_count = own_slots * dp
    keys = slot_count + rows
    bits = dp.bit_length() - 1
    key_block = max(256, own_slots)
    out_cols = model // tn
    vmem = pl.BlockSpec(memory_space=pltpu.VMEM)
    hbm = pl.BlockSpec(memory_space=pl.ANY)
    dma = pltpu.SemaphoreType.DMA
    outs = pl.pallas_call(
        functools.partial(layer_kernel, dp, tn, key_block),
        out_shape=(
            jax.ShapeDtypeStruct((rows, out_cols), BF16),
            jax.ShapeDtypeStruct((rows, head_cols), BF16),
            jax.ShapeDtypeStruct((2, rows, HD), BF16),
            jax.ShapeDtypeStruct((2, own_slots, HD), F32),
        ),
        in_specs=[pl.BlockSpec(memory_space=pltpu.SMEM), vmem, vmem, vmem, hbm, hbm],
        out_specs=(vmem,) * 4,
        scratch_shapes=[
            pltpu.VMEM((dp, units, depth, width), BF16),
            pltpu.VMEM((rows, model), BF16),
            pltpu.VMEM((tn, rows, out_cols), BF16),
            pltpu.VMEM((tn + 1, rows, out_cols), BF16),
            pltpu.VMEM((2, keys, HD), BF16),
            pltpu.VMEM((HD, keys), BF16),
            pltpu.VMEM((HD, keys), BF16),
            pltpu.VMEM((heads, rows, HD), BF16),
            pltpu.VMEM((heads, rows, HD), BF16),
            pltpu.VMEM((rows, head_cols), BF16),
            pltpu.VMEM((rows, head_cols), F32),
            pltpu.VMEM((heads, HD, rows), F32),
            pltpu.VMEM((heads, 1, rows), F32),
            pltpu.VMEM((heads, 1, rows), F32),
            pltpu.VMEM((heads, 1, rows), F32),
            pltpu.VMEM((2, slot_count, HD), BF16),
            pltpu.VMEM((2, slot_count, HD), BF16),
            pltpu.VMEM((2, key_block, HD), F32),
            dma((units,)),
            dma(()),
            dma((dp,)),
            dma((dp,)),
            dma((dp,)),
            dma((dp, units, bits)),
            dma((dp, units)),
            dma((tn,)),
            dma((tn + 1, dp // tn * units)),
            dma((dp,)),
            dma((dp,)),
        ],
        compiler_params=pltpu.CompilerParams(
            collective_id=0, has_side_effects=True, vmem_limit_bytes=60 * 1024 * 1024),
        name="layer",
    )(
        lengths, queries, jnp.transpose(token_kv, (1, 0, 2)),
        jnp.transpose(slot_cache, (1, 0, 2)), upstream, out_weight,
    )
    layer_output, query_grad, token_grad, slot_grad = outs
    return (
        layer_output, query_grad,
        jnp.transpose(token_grad, (1, 0, 2)), jnp.transpose(slot_grad, (1, 0, 2)),
    )


def solution(mesh):
    return jax.shard_map(
        functools.partial(on_device, mesh.shape["dp"], mesh.shape["tensor"]),
        mesh=mesh,
        in_specs=(
            P("dp", "tensor"),
            P("dp", None, "tensor"),
            P("dp", None, "tensor"),
            P("dp"),
            P("dp", None),
            P("tensor", "dp"),
        ),
        out_specs=(
            P("dp", "tensor"),
            P("dp", "tensor"),
            P("dp", None, "tensor"),
            P("dp", None, "tensor"),
        ),
        check_vma=False,
    )
```
